32 devices in a mesh: group: 2 (over x), example: 16 (over z, y, core).
Axes of the slice: x: 2, y: 2, z: 4, core: 2. Of those that a mesh axis runs over, the one named last changes fastest.
Arguments:
- train_grads: bfloat16 [32768, 4096], P(('group', 'example')), parts along dimension 0, may hold values from -6 to 6
- query_grads: bfloat16 [6144, 4096], P(('group', 'example')), parts along dimension 0, may hold values from -6 to 6
- left_inverse: bfloat16 [2, 64, 64], P('group'), parts along dimension 0, may hold values from -0.75 to 0.75
- right_inverse: bfloat16 [2, 64, 64], P('group'), parts along dimension 0, may hold values from -0.75 to 0.75
Outputs:
- scores: float32 [32768, 768], P(('group', 'example')), parts along dimension 0
- query_mass: float32 [6144, 1], P(('group', 'example')), parts along dimension 0
The draws below stay inside these ranges and needn't reach their ends.
There are 2 independent parts, one for each index of `group`. The reference program is written for one: setup_inputs(seed, part) draws one part's arguments, and reference() takes and returns one part's arrays. A program takes and returns all parts, laid end to end along the dimension named above; each array names one. Nothing has to cross between parts.
All inputs are finite; a program needn't handle non-finite values.
Results may differ from the reference program's by a relative error of at most 0.0041.
Values may be sent and summed in bfloat16 or wider, within the bound.
A program may use at most 64 MiB of HBM per device.

```python
import jax
import jax.numpy as jnp
from jax import lax

SIDE = 64
MDIM = 4096
MODS = 1
EX_DEV = 1024
QB_DEV = 192
SHIFTS = 3
EXAMPLES = 16384
QUERIES = 3072
N_EXAMPLE = 16


def block_scale(stream_key, extent, shards, smallest, largest):
    level, own = 1.0, jax.random.fold_in(stream_key, 6)
    for position, blocks in shards:
        heights = jnp.exp(jax.random.uniform(jax.random.fold_in(own, position), (blocks,), jnp.float32, smallest / len(shards), largest / len(shards)))
        level = level * jnp.repeat(heights, extent[position] // blocks).reshape([-1 if axis == position else 1 for axis in range(len(extent))])
    return level


def noise(key, extent, scale, limit, shards=(), kind=jnp.bfloat16):
    level = block_scale(key, extent, shards, -0.22, 0.18) if shards else 1.0
    drawn = jax.random.normal(key, extent, jnp.float32) * scale * level
    return jnp.minimum(jnp.maximum(drawn, -limit), limit).astype(kind)


def setup_inputs(seed: int = 0, part: int = 0) -> dict:
    arg_keys = jax.random.split(jax.random.key(seed), 5)
    part_splits = jax.random.split(jax.random.fold_in(arg_keys[4], part), 5)
    train_grads = noise(part_splits[0], (EXAMPLES, MODS * MDIM), 1.0, 6.0, ((0, 16),))
    query_grads = noise(part_splits[1], (QUERIES, MODS * MDIM), 1.0, 6.0, ((0, 16),))
    left_inverse = noise(part_splits[2], (MODS, SIDE, SIDE), SIDE ** -0.5, 0.75)
    right_inverse = noise(part_splits[3], (MODS, SIDE, SIDE), SIDE ** -0.5, 0.75)
    return {"train_grads": train_grads, "query_grads": query_grads, "left_inverse": left_inverse, "right_inverse": right_inverse}


def precondition(query_grads, left_inverse, right_inverse):
    count = query_grads.shape[0]
    mats = query_grads.reshape(count, MODS, SIDE, SIDE).astype(jnp.float32)
    inner = jnp.einsum('mab,qmbc->qmac', left_inverse.astype(jnp.float32), mats).astype(jnp.bfloat16)
    outer = jnp.einsum('qmac,mcd->qmad', inner.astype(jnp.float32), right_inverse.astype(jnp.float32))
    return outer.reshape(count, MODS * MDIM).astype(jnp.bfloat16)

def reference(train_grads, query_grads, left_inverse, right_inverse):
    count = N_EXAMPLE
    precond = precondition(query_grads, left_inverse, right_inverse)
    blocks = precond.reshape(count, QB_DEV, MODS * MDIM)
    slabs = train_grads.reshape(count, EX_DEV, MODS * MDIM)
    scale = 1.0 / jnp.sqrt(jnp.float32(MDIM))
    indices = jnp.arange(count, dtype=jnp.int32)

    def one_slab(index):
        slab = slabs[index]
        columns = []
        masses = []
        for shift_step in range(SHIFTS + 1):
            source = ((index - shift_step) % count).astype(jnp.int32)
            block = blocks[source]
            total = jnp.zeros((EX_DEV, QB_DEV), jnp.float32)
            module_mass = []
            for module in range(MODS):
                lo = module * MDIM
                part = jnp.dot(slab[:, lo:lo + MDIM], block[:, lo:lo + MDIM].T, preferred_element_type=jnp.float32) * scale
                total = total + part
                module_mass.append(lax.optimization_barrier(jnp.sum(part * part, axis=0)))
            columns.append(total)
            masses.append(jnp.stack(module_mass, axis=1))
        return (jnp.concatenate(columns, axis=1), jnp.stack(masses, axis=0))
    score_slabs, partials = lax.map(one_slab, indices)
    scores = score_slabs.reshape(count * EX_DEV, (SHIFTS + 1) * QB_DEV)
    mass = jnp.zeros((count, QB_DEV, MODS), jnp.float32)
    for shift_step in range(SHIFTS + 1):
        mass = mass + jnp.roll(partials[:, shift_step], -shift_step, axis=0)
    mass = mass / jnp.float32((SHIFTS + 1) * EX_DEV)
    return (scores, mass.reshape(count * QB_DEV, MODS))
```

```python
import functools
import math

import jax
import jax.numpy as jnp
from jax import lax
from jax.experimental import pallas as pl
from jax.experimental.pallas import tpu as pltpu
from jax.sharding import PartitionSpec as P

SHIFTS = 3
SLOTS = SHIFTS + 1
WIDTH = 256
AHEAD = 4
RELAY = 1
ROWS = 256

F32 = jnp.float32
BF16 = jnp.bfloat16


def kernel(
    count, train_hbm, query_ref, left_ref, right_ref, scores_ref, mass_ref,
    train, spread, right_blocks, blocks, sums, visiting, train_sem, send_sem, recv_sem, sums_send, sums_recv,
):
    me = lax.axis_index("example")
    chip = me // 2
    first_core = lax.rem(me, 2) == 0
    odd_chip = lax.rem(chip, 2) == 1
    chunks, _, width = blocks.shape
    qrows = query_ref.shape[0]
    side = left_ref.shape[1]
    rows = train.shape[0]
    per = width // side
    scale = 1.0 / math.sqrt(side * side)

    def at(steps):
        return {"example": lax.rem(me + steps + count, count)}

    def slot(chunk, index):
        return blocks.at[chunk, pl.ds(index * qrows, qrows), :]

    def copy(chunk, source, steps, target, sem):
        return pltpu.make_async_remote_copy(
            src_ref=slot(chunk, source),
            dst_ref=slot(chunk, target),
            send_sem=send_sem.at[chunk, sem],
            recv_sem=recv_sem.at[chunk, target],
            device_id=at(steps),
            device_id_type=pl.DeviceIdType.MESH,
        )

    load = pltpu.make_async_copy(train_hbm, train, train_sem)
    load.start()
    barrier = pltpu.get_barrier_semaphore()
    for steps in (-3, -2, -1, 1, 2, 3):
        pl.semaphore_signal(barrier, inc=1, device_id=at(steps), device_id_type=pl.DeviceIdType.MESH)

    right_blocks[...] = jnp.zeros_like(right_blocks)
    for i in range(per):
        right_blocks[i * side:(i + 1) * side, i * side:(i + 1) * side] = right_ref[0]
    row_c = lax.broadcasted_iota(jnp.int32, (side, width), 0)
    lane = lax.broadcasted_iota(jnp.int32, (side, width), 1)
    same_c = row_c == lax.rem(lane, side)

    def produce(chunk):
        pick = (row_c == lane // side + chunk * per).astype(F32).astype(BF16)
        wide = lax.dot_general(left_ref[0], pick, (((0,), (0,)), ((), ())), preferred_element_type=F32)
        for b in range(side):
            value = jnp.broadcast_to(wide[b:b + 1, :], (side, width))
            spread[b * side:(b + 1) * side, :] = jnp.where(same_c, value, 0.0).astype(BF16)
        inner = jnp.dot(query_ref[...], spread[...], preferred_element_type=F32).astype(BF16)
        outer = jnp.dot(inner, right_blocks[...], preferred_element_type=F32)
        blocks[chunk, 0:qrows, :] = outer.astype(BF16)

    def send(chunk):
        @pl.when(first_core)
        def _():
            copy(chunk, 0, 2, 2, 1).start()
            copy(chunk, 0, 1, 1, 0).start()

        @pl.when(jnp.logical_not(first_core))
        def _():
            copy(chunk, 0, 3, 3, 0).start()

            @pl.when(jnp.logical_not(odd_chip))
            def _():
                copy(chunk, 0, 1, 1, 1).start()

    def relay(chunk):
        @pl.when(first_core)
        def _():
            copy(chunk, 0, 3, 3, 0).wait_recv()

            @pl.when(odd_chip)
            def _():
                copy(chunk, 3, -2, 1, 4).start()

    def gather(chunk):
        @pl.when(first_core)
        def _():
            copy(chunk, 0, 2, 2, 1).wait_recv()
            copy(chunk, 2, 1, 3, 3).start()
            copy(chunk, 0, 1, 1, 0).wait_recv()
            copy(chunk, 1, 1, 2, 2).start()

        @pl.when(jnp.logical_not(first_core))
        def _():
            for index in range(1, SLOTS):
                copy(chunk, 0, 1, index, 0).wait_recv()

    def finish(chunk):
        @pl.when(first_core)
        def _():
            for sem in range(4):
                copy(chunk, 0, 1, 1, sem).wait_send()

            @pl.when(odd_chip)
            def _():
                copy(chunk, 0, 1, 1, 4).wait_send()

        @pl.when(jnp.logical_not(first_core))
        def _():
            copy(chunk, 0, 1, 1, 0).wait_send()

            @pl.when(jnp.logical_not(odd_chip))
            def _():
                copy(chunk, 0, 1, 1, 1).wait_send()

    def product(chunk, row):
        columns = pl.ds(pl.multiple_of(chunk * width, width), width)
        return lax.dot_general(
            train[row:row + ROWS, columns], blocks[chunk], (((1,), (1,)), ((), ())), preferred_element_type=F32
        )

    produce(0)
    pl.semaphore_wait(barrier, 6)
    send(0)

    @pl.loop(1, AHEAD)
    def _(chunk):
        produce(chunk)
        send(chunk)

    scores_ref[...] = jnp.zeros_like(scores_ref)
    load.wait()
    for chunk in range(RELAY):
        relay(chunk)

    @pl.loop(0, chunks - 1)
    def _(chunk):
        @pl.when(chunk + AHEAD < chunks)
        def _():
            produce(chunk + AHEAD)
            send(chunk + AHEAD)

        @pl.when(chunk + RELAY < chunks)
        def _():
            relay(chunk + RELAY)

        gather(chunk)
        for row in range(0, rows, ROWS):
            scores_ref[row:row + ROWS, :] += product(chunk, row)

    gather(chunks - 1)
    total = jnp.zeros((1, SLOTS * qrows), F32)
    for row in range(0, rows, ROWS):
        part = (scores_ref[row:row + ROWS, :] + product(chunks - 1, row)) * scale
        scores_ref[row:row + ROWS, :] = part
        total = total + jnp.sum(part * part, axis=0, keepdims=True)
    for index in range(SLOTS):
        sums[index] = jnp.broadcast_to(total[:, index * qrows:(index + 1) * qrows], sums.shape[1:])
    returns = [
        pltpu.make_async_remote_copy(
            src_ref=sums.at[index],
            dst_ref=visiting.at[index],
            send_sem=sums_send.at[index],
            recv_sem=sums_recv.at[index],
            device_id=at(-index),
            device_id_type=pl.DeviceIdType.MESH,
        )
        for index in range(1, SLOTS)
    ]
    for back in returns:
        back.start()

    @pl.loop(0, chunks)
    def _(chunk):
        finish(chunk)

    for back in returns:
        back.wait()
    mass = sums[0] + visiting[1] + visiting[2] + visiting[3]
    mass_ref[...] = jnp.transpose(mass)[:, 0:1] / F32(SLOTS * rows)


def local(count, train_grads, query_grads, left_inverse, right_inverse):
    rows, mdim = train_grads.shape
    qrows = query_grads.shape[0]
    chunks = mdim // WIDTH
    vmem = pl.BlockSpec(memory_space=pltpu.VMEM)
    return pl.pallas_call(
        functools.partial(kernel, count),
        out_shape=(
            jax.ShapeDtypeStruct((rows, SLOTS * qrows), F32),
            jax.ShapeDtypeStruct((qrows, 1), F32),
        ),
        in_specs=[pl.BlockSpec(memory_space=pl.ANY), vmem, vmem, vmem],
        out_specs=(vmem, vmem),
        scratch_shapes=[
            pltpu.VMEM((rows, mdim), BF16),
            pltpu.VMEM((mdim, WIDTH), BF16),
            pltpu.VMEM((WIDTH, WIDTH), BF16),
            pltpu.VMEM((chunks, SLOTS * qrows, WIDTH), BF16),
            pltpu.VMEM((SLOTS, 8, qrows), F32),
            pltpu.VMEM((SLOTS, 8, qrows), F32),
            pltpu.SemaphoreType.DMA,
            pltpu.SemaphoreType.DMA((chunks, 5)),
            pltpu.SemaphoreType.DMA((chunks, SLOTS)),
            pltpu.SemaphoreType.DMA((SLOTS,)),
            pltpu.SemaphoreType.DMA((SLOTS,)),
        ],
        compiler_params=pltpu.CompilerParams(
            collective_id=0, has_side_effects=True, vmem_limit_bytes=40 * 1024 * 1024
        ),
    )(train_grads, query_grads, left_inverse, right_inverse)


def solution(mesh):
    return jax.shard_map(
        functools.partial(local, mesh.shape["example"]),
        mesh=mesh,
        in_specs=(
            P(("group", "example"), None),
            P(("group", "example"), None),
            P("group", None, None),
            P("group", None, None),
        ),
        out_specs=(P(("group", "example"), None), P(("group", "example"), None)),
        check_vma=False,
    )
```

```python
import functools
import math

import jax
import jax.numpy as jnp
from jax import lax
from jax.experimental import pallas as pl
from jax.experimental.pallas import tpu as pltpu
from jax.sharding import PartitionSpec as P

SHIFTS = 3
SLOTS = SHIFTS + 1
WIDTH = 256
PIECES = 1
AHEAD = 4
VMEM_KIB = 58000
ROWS = 256

F32 = jnp.float32
BF16 = jnp.bfloat16


def kernel(
    count, train_hbm, query_hbm, left_hbm, right_hbm, scores_ref, mass_ref,
    train, query_ref, left_ref, right_ref, spread, right_blocks, blocks, sums, visiting, load_sem, send_sem, recv_sem, sums_send, sums_recv,
):
    me = lax.axis_index("example")
    chip = me // 2
    first_core = lax.rem(me, 2) == 0
    odd_chip = lax.rem(chip, 2) == 1
    chunks, _, width = blocks.shape
    qrows = query_ref.shape[0]
    prows = qrows // PIECES
    side = left_ref.shape[1]
    rows = train.shape[0]
    per = width // side
    scale = 1.0 / math.sqrt(side * side)

    def at(steps):
        return {"example": lax.rem(me + steps + count, count)}

    def slot(chunk, piece, index):
        return blocks.at[chunk, pl.ds(index * qrows + piece * prows, prows), :]

    def copy(chunk, piece, source, steps, target, sem):
        unit = chunk * PIECES + piece
        return pltpu.make_async_remote_copy(
            src_ref=slot(chunk, piece, source),
            dst_ref=slot(chunk, piece, target),
            send_sem=send_sem.at[unit, sem],
            recv_sem=recv_sem.at[unit, target],
            device_id=at(steps),
            device_id_type=pl.DeviceIdType.MESH,
        )

    barrier = pltpu.get_barrier_semaphore()
    for steps in (-3, -2, -1, 1, 2, 3):
        pl.semaphore_signal(barrier, inc=1, device_id=at(steps), device_id_type=pl.DeviceIdType.MESH)
    loads = [
        pltpu.make_async_copy(source, target, load_sem.at[index])
        for index, (source, target) in enumerate(
            ((left_hbm, left_ref), (right_hbm, right_ref), (query_hbm, query_ref), (train_hbm, train))
        )
    ]
    for load in loads:
        load.start()

    row_c = lax.broadcasted_iota(jnp.int32, (side, width), 0)
    lane = lax.broadcasted_iota(jnp.int32, (side, width), 1)
    same_c = row_c == lax.rem(lane, side)

    def build(chunk):
        pick = (row_c == lane // side + chunk * per).astype(F32).astype(BF16)
        wide = lax.dot_general(left_ref[0], pick, (((0,), (0,)), ((), ())), preferred_element_type=F32)
        for b in range(side):
            value = jnp.broadcast_to(wide[b:b + 1, :], (side, width))
            spread[b * side:(b + 1) * side, :] = jnp.where(same_c, value, 0.0).astype(BF16)

    def apply(chunk):
        inner = jnp.dot(query_ref[...], spread[...], preferred_element_type=F32).astype(BF16)
        outer = jnp.dot(inner, right_blocks[...], preferred_element_type=F32)
        blocks[chunk, 0:qrows, :] = outer.astype(BF16)

    def send(chunk):
        @pl.when(first_core)
        def _():
            for piece in range(PIECES):
                copy(chunk, piece, 0, 2, 2, 1).start()
                copy(chunk, piece, 0, 1, 1, 0).start()

        @pl.when(jnp.logical_not(first_core))
        def _():
            for piece in range(PIECES):
                copy(chunk, piece, 0, 3, 3, 0).start()

                @pl.when(jnp.logical_not(odd_chip))
                def _():
                    copy(chunk, piece, 0, 1, 1, 1).start()

    def relay(chunk):
        @pl.when(first_core)
        def _():
            for piece in range(PIECES):
                copy(chunk, piece, 0, 3, 3, 0).wait_recv()

                @pl.when(odd_chip)
                def _():
                    copy(chunk, piece, 3, -2, 1, 4).start()

    def gather(chunk):
        @pl.when(first_core)
        def _():
            for piece in range(PIECES):
                copy(chunk, piece, 0, 2, 2, 1).wait_recv()
                copy(chunk, piece, 2, 1, 3, 3).start()
                copy(chunk, piece, 0, 1, 1, 0).wait_recv()
                copy(chunk, piece, 1, 1, 2, 2).start()

        gather_near(chunk)

    def gather_near(chunk):
        @pl.when(jnp.logical_not(first_core))
        def _():
            for piece in range(PIECES):
                copy(chunk, piece, 0, 1, 1, 0).wait_recv()

    def gather_far(chunk):
        @pl.when(jnp.logical_not(first_core))
        def _():
            for piece in range(PIECES):
                for index in range(2, SLOTS):
                    copy(chunk, piece, 0, 1, index, 0).wait_recv()

    def finish(chunk):
        for piece in range(PIECES):
            @pl.when(first_core)
            def _():
                for sem in range(4):
                    copy(chunk, piece, 0, 1, 1, sem).wait_send()

                @pl.when(odd_chip)
                def _():
                    copy(chunk, piece, 0, 1, 1, 4).wait_send()

            @pl.when(jnp.logical_not(first_core))
            def _():
                copy(chunk, piece, 0, 1, 1, 0).wait_send()

                @pl.when(jnp.logical_not(odd_chip))
                def _():
                    copy(chunk, piece, 0, 1, 1, 1).wait_send()

    def product(chunk, row, first, last):
        columns = pl.ds(pl.multiple_of(chunk * width, width), width)
        return lax.dot_general(
            train[row:row + ROWS, columns], blocks[chunk, first:last, :], (((1,), (1,)), ((), ())),
            preferred_element_type=F32,
        )

    loads[0].wait()
    build(0)
    right_blocks[...] = jnp.zeros_like(right_blocks)
    for load in loads[1:3]:
        load.wait()
    for i in range(per):
        right_blocks[i * side:(i + 1) * side, i * side:(i + 1) * side] = right_ref[0]
    apply(0)
    pl.semaphore_wait(barrier, 6)
    send(0)

    @pl.loop(1, AHEAD)
    def _(chunk):
        build(chunk)
        apply(chunk)
        send(chunk)

    scores_ref[...] = jnp.zeros_like(scores_ref)
    loads[3].wait()
    relay(0)
    every = SLOTS * qrows

    @pl.loop(0, chunks // 2 - 1)
    def _(pair):
        chunk = pair * 2

        @pl.when(chunk + AHEAD < chunks)
        def _():
            for later in (chunk + AHEAD, chunk + AHEAD + 1):
                build(later)
                apply(later)
                send(later)

        for now in (chunk, chunk + 1):
            relay(now + 1)
            gather(now)
            gather_far(now)
        for row in range(0, rows, ROWS):
            scores_ref[row:row + ROWS, :] += product(chunk, row, 0, every) + product(chunk + 1, row, 0, every)

    relay(chunks - 1)
    gather(chunks - 2)
    gather_far(chunks - 2)
    for row in range(0, rows, ROWS):
        scores_ref[row:row + ROWS, :] += product(chunks - 2, row, 0, every)

    def last(first, end):
        total = jnp.zeros((1, end - first), F32)
        for row in range(0, rows, ROWS):
            part = (scores_ref[row:row + ROWS, first:end] + product(chunks - 1, row, first, end)) * scale
            scores_ref[row:row + ROWS, first:end] = part
            total = total + jnp.sum(part * part, axis=0, keepdims=True)
        return total

    gather(chunks - 1)
    near = last(0, every // 2)
    gather_far(chunks - 1)
    total = jnp.concatenate([near, last(every // 2, every)], axis=1)
    for index in range(SLOTS):
        sums[index] = jnp.broadcast_to(total[:, index * qrows:(index + 1) * qrows], sums.shape[1:])
    returns = [
        pltpu.make_async_remote_copy(
            src_ref=sums.at[index],
            dst_ref=visiting.at[index],
            send_sem=sums_send.at[index],
            recv_sem=sums_recv.at[index],
            device_id=at(-index),
            device_id_type=pl.DeviceIdType.MESH,
        )
        for index in range(1, SLOTS)
    ]
    for back in returns:
        back.start()

    @pl.loop(0, chunks)
    def _(chunk):
        finish(chunk)

    for back in returns:
        back.wait()
    mass = sums[0] + visiting[1] + visiting[2] + visiting[3]
    mass_ref[...] = mass[0:1, :] / F32(SLOTS * rows)


def local(count, train_grads, query_grads, left_inverse, right_inverse):
    rows, mdim = train_grads.shape
    qrows = query_grads.shape[0]
    chunks = mdim // WIDTH
    vmem = pl.BlockSpec(memory_space=pltpu.VMEM)
    scores, mass = pl.pallas_call(
        functools.partial(kernel, count),
        out_shape=(
            pltpu.VMEM((rows, SLOTS * qrows), F32),
            jax.ShapeDtypeStruct((1, qrows), F32),
        ),
        in_specs=[pl.BlockSpec(memory_space=pl.ANY)] * 4,
        out_specs=(vmem, vmem),
        scratch_shapes=[
            pltpu.VMEM((rows, mdim), BF16),
            pltpu.VMEM((qrows, mdim), BF16),
            pltpu.VMEM(left_inverse.shape, BF16),
            pltpu.VMEM(right_inverse.shape, BF16),
            pltpu.VMEM((mdim, WIDTH), BF16),
            pltpu.VMEM((WIDTH, WIDTH), BF16),
            pltpu.VMEM((chunks, SLOTS * qrows, WIDTH), BF16),
            pltpu.VMEM((SLOTS, 8, qrows), F32),
            pltpu.VMEM((SLOTS, 8, qrows), F32),
            pltpu.SemaphoreType.DMA((4,)),
            pltpu.SemaphoreType.DMA((chunks * PIECES, 5)),
            pltpu.SemaphoreType.DMA((chunks * PIECES, SLOTS)),
            pltpu.SemaphoreType.DMA((SLOTS,)),
            pltpu.SemaphoreType.DMA((SLOTS,)),
        ],
        compiler_params=pltpu.CompilerParams(
            collective_id=0, has_side_effects=True, vmem_limit_bytes=VMEM_KIB * 1024
        ),
    )(train_grads, query_grads, left_inverse, right_inverse)
    return scores, mass.reshape(qrows, 1)


def solution(mesh):
    return jax.shard_map(
        functools.partial(local, mesh.shape["example"]),
        mesh=mesh,
        in_specs=(
            P(("group", "example"), None),
            P(("group", "example"), None),
            P("group", None, None),
            P("group", None, None),
        ),
        out_specs=(P(("group", "example"), None), P(("group", "example"), None)),
        check_vma=False,
    )
```

```python
import functools
import math

import jax
import jax.numpy as jnp
from jax import lax
from jax.experimental import pallas as pl
from jax.experimental.pallas import tpu as pltpu
from jax.sharding import PartitionSpec as P

SHIFTS = 3
SLOTS = SHIFTS + 1
WIDTH = 256
PIECES = 1
AHEAD = 4
VMEM_KIB = 58000
ROWS = 256

F32 = jnp.float32
BF16 = jnp.bfloat16


def kernel(
    count, train_hbm, query_hbm, left_hbm, right_hbm, scores_ref, mass_ref,
    train, query_ref, left_ref, right_ref, spread, right_blocks, blocks, sums, visiting, load_sem, send_sem, recv_sem, sums_send, sums_recv,
):
    me = lax.axis_index("example")
    chip = me // 2
    first_core = lax.rem(me, 2) == 0
    odd_chip = lax.rem(chip, 2) == 1
    chunks, _, width = blocks.shape
    qrows = query_ref.shape[0]
    prows = qrows // PIECES
    side = left_ref.shape[1]
    rows = train.shape[0]
    per = width // side
    scale = 1.0 / math.sqrt(side * side)

    def at(steps):
        return {"example": lax.rem(me + steps + count, count)}

    def slot(chunk, piece, index):
        return blocks.at[chunk, pl.ds(index * qrows + piece * prows, prows), :]

    def copy(chunk, piece, source, steps, target, sem):
        unit = chunk * PIECES + piece
        return pltpu.make_async_remote_copy(
            src_ref=slot(chunk, piece, source),
            dst_ref=slot(chunk, piece, target),
            send_sem=send_sem.at[unit, sem],
            recv_sem=recv_sem.at[unit, target],
            device_id=at(steps),
            device_id_type=pl.DeviceIdType.MESH,
        )

    barrier = pltpu.get_barrier_semaphore()
    for steps in (-3, -2, -1, 1, 2, 3):
        pl.semaphore_signal(barrier, inc=1, device_id=at(steps), device_id_type=pl.DeviceIdType.MESH)
    loads = [
        pltpu.make_async_copy(source, target, load_sem.at[index])
        for index, (source, target) in enumerate(
            ((left_hbm, left_ref), (right_hbm, right_ref), (query_hbm, query_ref), (train_hbm, train))
        )
    ]
    for load in loads:
        load.start()

    row_c = lax.broadcasted_iota(jnp.int32, (side, width), 0)
    lane = lax.broadcasted_iota(jnp.int32, (side, width), 1)
    same_c = row_c == lax.rem(lane, side)

    def build(chunk):
        pick = (row_c == lane // side + chunk * per).astype(F32).astype(BF16)
        wide = lax.dot_general(left_ref[0], pick, (((0,), (0,)), ((), ())), preferred_element_type=F32)
        for b in range(side):
            value = jnp.broadcast_to(wide[b:b + 1, :], (side, width))
            spread[b * side:(b + 1) * side, :] = jnp.where(same_c, value, 0.0).astype(BF16)

    def apply(chunk):
        inner = jnp.dot(query_ref[...], spread[...], preferred_element_type=F32).astype(BF16)
        outer = jnp.dot(inner, right_blocks[...], preferred_element_type=F32)
        blocks[chunk, 0:qrows, :] = outer.astype(BF16)

    def send(chunk):
        @pl.when(first_core)
        def _():
            for piece in range(PIECES):
                copy(chunk, piece, 0, 2, 2, 1).start()
                copy(chunk, piece, 0, 1, 1, 0).start()

        @pl.when(jnp.logical_not(first_core))
        def _():
            for piece in range(PIECES):
                copy(chunk, piece, 0, 3, 3, 0).start()

                @pl.when(jnp.logical_not(odd_chip))
                def _():
                    copy(chunk, piece, 0, 1, 1, 1).start()

    def relay(chunk):
        @pl.when(first_core)
        def _():
            for piece in range(PIECES):
                copy(chunk, piece, 0, 3, 3, 0).wait_recv()

                @pl.when(odd_chip)
                def _():
                    copy(chunk, piece, 3, -2, 1, 4).start()

    def gather(chunk):
        @pl.when(first_core)
        def _():
            for piece in range(PIECES):
                copy(chunk, piece, 0, 2, 2, 1).wait_recv()
                copy(chunk, piece, 2, 1, 3, 3).start()
                copy(chunk, piece, 0, 1, 1, 0).wait_recv()
                copy(chunk, piece, 1, 1, 2, 2).start()

        gather_near(chunk)

    def gather_near(chunk):
        @pl.when(jnp.logical_not(first_core))
        def _():
            for piece in range(PIECES):
                copy(chunk, piece, 0, 1, 1, 0).wait_recv()

    def gather_far(chunk):
        @pl.when(jnp.logical_not(first_core))
        def _():
            for piece in range(PIECES):
                for index in range(2, SLOTS):
                    copy(chunk, piece, 0, 1, index, 0).wait_recv()

    def finish(chunk):
        for piece in range(PIECES):
            @pl.when(first_core)
            def _():
                for sem in range(4):
                    copy(chunk, piece, 0, 1, 1, sem).wait_send()

                @pl.when(odd_chip)
                def _():
                    copy(chunk, piece, 0, 1, 1, 4).wait_send()

            @pl.when(jnp.logical_not(first_core))
            def _():
                copy(chunk, piece, 0, 1, 1, 0).wait_send()

                @pl.when(jnp.logical_not(odd_chip))
                def _():
                    copy(chunk, piece, 0, 1, 1, 1).wait_send()

    def product(chunk, row, first, last):
        columns = pl.ds(pl.multiple_of(chunk * width, width), width)
        return lax.dot_general(
            train[row:row + ROWS, columns], blocks[chunk, first:last, :], (((1,), (1,)), ((), ())),
            preferred_element_type=F32,
        )

    loads[0].wait()
    build(0)
    right_blocks[...] = jnp.zeros_like(right_blocks)
    for load in loads[1:3]:
        load.wait()
    for i in range(per):
        right_blocks[i * side:(i + 1) * side, i * side:(i + 1) * side] = right_ref[0]
    apply(0)
    pl.semaphore_wait(barrier, 6)
    send(0)

    @pl.loop(1, AHEAD)
    def _(chunk):
        build(chunk)
        apply(chunk)
        send(chunk)

    scores_ref[...] = jnp.zeros_like(scores_ref)
    loads[3].wait()
    relay(0)
    every = SLOTS * qrows

    @pl.loop(0, chunks // 2 - 1)
    def _(pair):
        chunk = pair * 2

        for now in (chunk, chunk + 1):
            @pl.when(now + AHEAD < chunks)
            def _():
                build(now + AHEAD)
                apply(now + AHEAD)
                send(now + AHEAD)

            relay(now + 1)
            gather(now)
            gather_far(now)
            for row in range(0, rows, ROWS):
                scores_ref[row:row + ROWS, :] += product(now, row, 0, every)

    relay(chunks - 1)
    gather(chunks - 2)
    gather_far(chunks - 2)
    for row in range(0, rows, ROWS):
        scores_ref[row:row + ROWS, :] += product(chunks - 2, row, 0, every)

    def last(first, end):
        total = jnp.zeros((1, end - first), F32)
        for row in range(0, rows, ROWS):
            part = (scores_ref[row:row + ROWS, first:end] + product(chunks - 1, row, first, end)) * scale
            scores_ref[row:row + ROWS, first:end] = part
            total = total + jnp.sum(part * part, axis=0, keepdims=True)
        return total

    gather(chunks - 1)
    near = last(0, every // 2)
    gather_far(chunks - 1)
    total = jnp.concatenate([near, last(every // 2, every)], axis=1)
    for index in range(SLOTS):
        sums[index] = jnp.broadcast_to(total[:, index * qrows:(index + 1) * qrows], sums.shape[1:])
    returns = [
        pltpu.make_async_remote_copy(
            src_ref=sums.at[index],
            dst_ref=visiting.at[index],
            send_sem=sums_send.at[index],
            recv_sem=sums_recv.at[index],
            device_id=at(-index),
            device_id_type=pl.DeviceIdType.MESH,
        )
        for index in range(1, SLOTS)
    ]
    for back in returns:
        back.start()

    @pl.loop(0, chunks)
    def _(chunk):
        finish(chunk)

    for back in returns:
        back.wait()
    mass = sums[0] + visiting[1] + visiting[2] + visiting[3]
    mass_ref[...] = mass[0:1, :] / F32(SLOTS * rows)


def local(count, train_grads, query_grads, left_inverse, right_inverse):
    rows, mdim = train_grads.shape
    qrows = query_grads.shape[0]
    chunks = mdim // WIDTH
    vmem = pl.BlockSpec(memory_space=pltpu.VMEM)
    scores, mass = pl.pallas_call(
        functools.partial(kernel, count),
        out_shape=(
            pltpu.VMEM((rows, SLOTS * qrows), F32),
            jax.ShapeDtypeStruct((1, qrows), F32),
        ),
        in_specs=[pl.BlockSpec(memory_space=pl.ANY)] * 4,
        out_specs=(vmem, vmem),
        scratch_shapes=[
            pltpu.VMEM((rows, mdim), BF16),
            pltpu.VMEM((qrows, mdim), BF16),
            pltpu.VMEM(left_inverse.shape, BF16),
            pltpu.VMEM(right_inverse.shape, BF16),
            pltpu.VMEM((mdim, WIDTH), BF16),
            pltpu.VMEM((WIDTH, WIDTH), BF16),
            pltpu.VMEM((chunks, SLOTS * qrows, WIDTH), BF16),
            pltpu.VMEM((SLOTS, 8, qrows), F32),
            pltpu.VMEM((SLOTS, 8, qrows), F32),
            pltpu.SemaphoreType.DMA((4,)),
            pltpu.SemaphoreType.DMA((chunks * PIECES, 5)),
            pltpu.SemaphoreType.DMA((chunks * PIECES, SLOTS)),
            pltpu.SemaphoreType.DMA((SLOTS,)),
            pltpu.SemaphoreType.DMA((SLOTS,)),
        ],
        compiler_params=pltpu.CompilerParams(
            collective_id=0, has_side_effects=True, vmem_limit_bytes=VMEM_KIB * 1024
        ),
    )(train_grads, query_grads, left_inverse, right_inverse)
    return scores, mass.reshape(qrows, 1)


def solution(mesh):
    return jax.shard_map(
        functools.partial(local, mesh.shape["example"]),
        mesh=mesh,
        in_specs=(
            P(("group", "example"), None),
            P(("group", "example"), None),
            P("group", None, None),
            P("group", None, None),
        ),
        out_specs=(P(("group", "example"), None), P(("group", "example"), None)),
        check_vma=False,
    )
```
